128 devices in a mesh: row: 8 (over y, core), col: 16 (over x, z).
Axes of the slice: x: 4, y: 4, z: 4, core: 2. Of those that a mesh axis runs over, the one named last changes fastest.
Arguments:
- amplitudes: bfloat16 [12288, 8192], P(('row', 'col')), may hold values from -6 to 6
- integrals: bfloat16 [8192, 8192], P('row', 'col'), may hold values from -0.09375 to 0.09375
- amplitude_mask: int32 [12288, 64], P(('row', 'col')), may hold values from 0 to 1, as said below
- integral_mask: int32 [64, 64], P('row', 'col'), may hold values from 0 to 1
Outputs:
- ladder: bfloat16 [12288, 8192], P('row', 'col')
The draws below stay inside these ranges and needn't reach their ends.
Inputs may be any that keep to these rules, and one draw needn't show every extreme that they name: `amplitude_mask`: in every row the kept tiles form one cyclic band of consecutive tiles, 1 to 40 of them; some row keeps exactly 40.
All inputs are finite; a program needn't handle non-finite values.
Results may differ from the reference program's by a relative error of at most 0.001.
Values may be sent and summed in bfloat16 or wider, within the bound.
No kernel may reach another device: no remote copies, remote signals or barrier semaphores. Data moves between devices by JAX's collectives and lax.ppermute only.
A program may use at most 128 MiB of HBM per device.

```python
import jax
import jax.numpy as jnp

TILE = 128
KT = 64
PAIR_DEV = 96
KEEP = 40
KDIM = 8192
PAIRS = 12288


def draw_amplitude_mask(key, part):
    key = jax.random.fold_in(key, 11)
    keys = jax.random.split(key, 5)
    blocks = PAIRS // PAIR_DEV
    base = jax.random.randint(keys[0], (blocks,), KT * 3 // 16, KEEP + 1)
    counts = jnp.repeat(base, PAIR_DEV) + jax.random.randint(keys[1], (PAIRS,), -1, 2)
    counts = jnp.clip(counts, 1, KEEP)
    chosen = jax.random.randint(keys[2], (), 0, PAIRS)
    counts = jnp.where(jnp.arange(PAIRS) == chosen, KEEP, counts)
    start = jnp.repeat(jax.random.randint(keys[3], (blocks,), 0, KT), PAIR_DEV)
    start = start + jax.random.randint(keys[4], (PAIRS,), 0, 2)
    offset = (jnp.arange(KT)[None, :] - start[:, None]) % KT
    return (offset < counts[:, None]).astype(jnp.int32)


def draw_integral_mask(key, part):
    key = jax.random.fold_in(key, 23)
    rows = jnp.arange(KT)[:, None]
    cols = jnp.arange(KT)[None, :]
    apart = jnp.abs(rows - cols)
    apart = jnp.minimum(apart, KT - apart)
    limit = jnp.where(apart <= KT // 8, 9, 5)
    coins = jax.random.randint(key, (KT, KT), 0, 10)
    return (coins < limit).astype(jnp.int32)


def block_scale(key, extent, pieces, low, largest):
    loudness, own = 1.0, jax.random.fold_in(key, 6)
    for dim, blocks in pieces:
        heights = jnp.exp(jax.random.uniform(jax.random.fold_in(own, dim), (blocks,), jnp.float32, low / len(pieces), largest / len(pieces)))
        loudness = loudness * jnp.repeat(heights, extent[dim] // blocks).reshape([-1 if axis == dim else 1 for axis in range(len(extent))])
    return loudness


def noise(key, shape, width, reach, pieces=(), dtype=jnp.bfloat16):
    result = jax.random.normal(key, shape, jnp.float32) * width
    if len(pieces) > 0:
        result = block_scale(key, shape, pieces, -0.22, 0.18) * result
    return jnp.clip(result, min=-reach, max=reach).astype(dtype)


def setup_inputs(seed: int = 0) -> dict:
    seeds = jax.random.split(jax.random.key(seed), 5)
    amplitudes = noise(seeds[0], (PAIRS, KDIM), 1.0, 6.0, ((0, 128),))
    integrals = noise(seeds[1], (KDIM, KDIM), (KDIM // 2) ** -0.5, 0.09375, ((0, 8), (1, 16)))
    amplitude_mask = draw_amplitude_mask(jax.random.fold_in(seeds[4], 71), 0)
    integral_mask = draw_integral_mask(jax.random.fold_in(seeds[4], 71), 0)
    return {"amplitudes": amplitudes, "integrals": integrals, "amplitude_mask": amplitude_mask, "integral_mask": integral_mask}


def reference(amplitudes, integrals, amplitude_mask, integral_mask):
    amp_keep = jnp.repeat(amplitude_mask, TILE, axis=1).astype(jnp.bfloat16)
    kept_amps = amplitudes * amp_keep
    int_keep = jnp.repeat(jnp.repeat(integral_mask, TILE, axis=0), TILE, axis=1).astype(jnp.bfloat16)
    kept_ints = integrals * int_keep
    return jnp.dot(kept_amps, kept_ints, preferred_element_type=jnp.float32).astype(jnp.bfloat16)
```

```python
import functools

import jax
import jax.numpy as jnp
from jax import lax
from jax.experimental import pallas as pl
from jax.experimental.pallas import tpu as pltpu
from jax.sharding import PartitionSpec as P

TILE = 128
KT = 64
SLOTS = 40
FOLD = KT - SLOTS
WIDE = (SLOTS + 1) * TILE
BF = jnp.bfloat16


def pack_kernel(mask_ref, amps_ref, *outs):
    rows = amps_ref.shape[0]
    mask = mask_ref[...]
    tile = lax.broadcasted_iota(jnp.int32, mask.shape, 1)
    count = jnp.sum(mask, axis=1, keepdims=True)
    low = jnp.min(jnp.where(mask > 0, tile, KT), axis=1, keepdims=True)
    high = jnp.max(jnp.where(mask > 0, tile, -1), axis=1, keepdims=True)
    end = jnp.min(jnp.where(mask > 0, KT, tile), axis=1, keepdims=True)
    wraps = high - low + 1 > count
    alpha = jnp.where(wraps, 0, jnp.minimum(low, FOLD))
    beta = jnp.where(wraps, end, SLOTS)
    first = jnp.where(wraps, end + KT - count, low)
    last = jnp.where(wraps, KT, high + 1)
    wide = lambda v: jnp.broadcast_to(v.astype(jnp.float32), (rows, TILE)).astype(BF)
    code = wide(jnp.where(wraps, -end, alpha))
    alpha, beta, first, last = wide(alpha), wide(beta), wide(first), wide(last)
    zero = jnp.zeros((rows, TILE), BF)

    def tile_of(t):
        return amps_ref[:, t * TILE : (t + 1) * TILE]

    def put(j, value):
        row = 0
        for out in outs:
            n = out.shape[0]
            out[:, j * TILE : (j + 1) * TILE] = value[row : row + n]
            row += n

    for j in range(SLOTS):
        value = jnp.where((first <= j) & (j < last), tile_of(j), zero)
        value = jnp.where((beta < SLOTS) & (j < beta), tile_of(j), value)
        far = jnp.where((first <= j + FOLD) & (j + FOLD < last), tile_of(j + FOLD), zero)
        value = jnp.where(beta <= j, far, value)
        if j < FOLD:
            up = jnp.where((first <= j + SLOTS) & (j + SLOTS < last), tile_of(j + SLOTS), zero)
            value = jnp.where(j < alpha, up, value)
        put(j, value)
    put(SLOTS, code)


def ints_kernel(mask_ref, ints_ref, kept_ref):
    for i in range(ints_ref.shape[0] // TILE):
        for j in range(ints_ref.shape[1] // TILE):
            at = (slice(i * TILE, (i + 1) * TILE), slice(j * TILE, (j + 1) * TILE))
            keep = jnp.full((TILE, TILE), mask_ref[j, i].astype(jnp.float32), jnp.float32).astype(BF)
            kept_ref[at] = ints_ref[at] * keep


def mm_kernel(n_in, parts, *refs):
    offs = refs[0]
    amps = refs[1 : 1 + n_in]
    ints = refs[1 + n_in]
    out, wide, done, sem = refs[-4:]
    starts, at = [], 0
    for part in parts:
        starts.append(at)
        at += part[2]

    def place(part):
        return pl.multiple_of(offs[part[3]] + part[4], 16)

    for part, p in zip(parts, starts):
        a, row0, rows = part[:3]
        code = amps[a][row0 : row0 + rows, SLOTS * TILE :]
        zero = jnp.zeros((rows, TILE), BF)
        alpha = jnp.where(code < 0, zero, code)
        beta = jnp.where(code < 0, zero - code, zero + SLOTS)

        def slot(j):
            return amps[a][row0 : row0 + rows, j * TILE : (j + 1) * TILE]

        for t in range(KT):
            if t < FOLD:
                v = jnp.where((alpha <= t) & (t < beta), slot(t), zero)
            elif t < SLOTS:
                v = jnp.where(t < beta, slot(t), zero)
                v = jnp.where(beta <= t - FOLD, slot(t - FOLD), v)
            else:
                v = jnp.where(t - SLOTS < alpha, slot(t - SLOTS), zero)
                v = jnp.where(beta <= t - FOLD, slot(t - FOLD), v)
            wide[p : p + rows, t * TILE : (t + 1) * TILE] = v

    done[...] = jnp.dot(wide[...], ints[...], preferred_element_type=jnp.float32).astype(BF)
    copies = [
        pltpu.make_async_copy(done.at[pl.ds(p, part[2])], out.at[pl.ds(place(part), part[2])], sem)
        for part, p in zip(parts, starts)
    ]
    for c in copies:
        c.start()
    for c in copies:
        c.wait()


def multiply(amps, parts, offs, ints, out, out_rows):
    rows = sum(p[2] for p in parts)
    cols = ints.shape[1]
    whole = pl.BlockSpec(memory_space=pltpu.VMEM)
    in_specs = [pl.BlockSpec(memory_space=pltpu.SMEM)] + [whole] * (len(amps) + 1)
    args = [offs] + list(amps) + [ints]
    alias = {}
    if out is not None:
        in_specs.append(pl.BlockSpec(memory_space=pl.ANY))
        alias = {len(args): 0}
        args.append(out)
    return pl.pallas_call(
        functools.partial(mm_kernel, len(amps), tuple(parts)),
        out_shape=jax.ShapeDtypeStruct((out_rows, cols), BF),
        in_specs=in_specs,
        out_specs=pl.BlockSpec(memory_space=pl.ANY),
        scratch_shapes=[
            pltpu.VMEM((rows, KT * TILE), BF),
            pltpu.VMEM((rows, cols), BF),
            pltpu.SemaphoreType.DMA,
        ],
        input_output_aliases=alias,
        compiler_params=pltpu.CompilerParams(vmem_limit_bytes=14 * 2**20),
        cost_estimate=pl.CostEstimate(
            flops=2 * rows * KT * TILE * cols,
            bytes_accessed=2 * (rows * WIDE + KT * TILE * cols + rows * cols),
            transcendentals=0,
        ),
    )(*args)


def pack(mask, amps):
    rows = amps.shape[0]
    sizes = [rows]
    return pl.pallas_call(
        pack_kernel,
        out_shape=[jax.ShapeDtypeStruct((n, WIDE), BF) for n in sizes],
    )(mask, amps)


def mask_ints(mask, ints):
    return pl.pallas_call(
        ints_kernel,
        out_shape=jax.ShapeDtypeStruct(ints.shape, ints.dtype),
        in_specs=[pl.BlockSpec(memory_space=pltpu.SMEM), pl.BlockSpec(memory_space=pltpu.VMEM)],
        out_specs=pl.BlockSpec(memory_space=pltpu.VMEM),
    )(mask.T, ints)


def moves(nx, nz, n_row):
    def shift(dx, dz):
        pairs = []
        for r in range(n_row):
            s = 1 - 2 * (r % 2)
            for x in range(nx):
                for z in range(nz):
                    to = (x + s * dx) % nx * nz + (z + s * dz) % nz
                    pairs.append((r * nx * nz + x * nz + z, r * nx * nz + to))
        return pairs

    return shift(1, 0), shift(-1, 0), shift(0, 1), shift(0, -1)


def on_device(amplitudes, integrals, amplitude_mask, integral_mask):
    dev_rows = amplitudes.shape[0]
    own = pack(amplitude_mask, amplitudes)[0]
    kept_ints = mask_ints(integral_mask, integrals)
    all_ints = lax.all_gather(kept_ints, "row", axis=0, tiled=True)
    half = dev_rows // 2
    xf, xb, zf, zb = moves(4, 4, 8)
    go = lambda v, perm: lax.ppermute(v, ("row", "col"), perm)
    x_m, z_m = go(own, xf), go(own, zf)
    x_p, z_p = go(own, xb), go(own, zb)
    x2, mm = go(x_m, xf), go(x_m, zf)
    pm, pp = go(z_m, xb), go(x_p, zb)
    mp, z2 = go(z_p, xf), go(z_m, zf)
    x2p, pz2 = go(pp, xb), go(pp, zb)
    mz2, x2m = go(z2, xf), go(x2, zf)
    far_a, far_b = go(pz2[:half], xb), go(x2p[half:], zb)

    me = lax.axis_index("col")
    sign = 1 - 2 * (lax.axis_index("row") % 2)
    x, z = me // 4, me % 4
    at = lambda dx, dz: ((x + sign * dx + 4) % 4 * 4 + (z + sign * dz + 4) % 4) * dev_rows
    total = 16 * dev_rows

    def call(blocks, out):
        arrays = [b[0] for b in blocks]
        offs = jnp.stack([at(*b[1]) for b in blocks]).astype(jnp.int32)
        parts = [(i, 0, b[0].shape[0], i, b[2]) for i, b in enumerate(blocks)]
        return multiply(arrays, parts, offs, all_ints, out, total)

    out = call([(own, (0, 0), 0), (x_m, (-1, 0), 0), (z_m, (0, -1), 0), (x_p, (1, 0), 0), (z_p, (0, 1), 0)], None)
    out = call([(x2, (2, 0), 0), (mm, (-1, -1), 0), (pm, (1, -1), 0), (pp, (1, 1), 0)], out)
    out = call([(mp, (-1, 1), 0), (z2, (0, 2), 0), (x2p, (2, 1), 0), (pz2, (1, 2), 0)], out)
    out = call([(mz2, (-1, 2), 0), (x2m, (2, -1), 0), (far_a, (2, 2), 0), (far_b, (2, 2), half)], out)
    return out


def solution(mesh):
    in_specs = (P(("row", "col"), None), P("row", "col"), P(("row", "col"), None), P("row", "col"))
    out_specs = P("row", "col")
    return jax.shard_map(
        on_device, mesh=mesh, in_specs=in_specs, out_specs=out_specs, check_vma=False
    )
```

```python
import functools

import jax
import jax.numpy as jnp
from jax import lax
from jax.experimental import pallas as pl
from jax.experimental.pallas import tpu as pltpu
from jax.sharding import PartitionSpec as P

TILE = 128
KT = 64
SLOTS = 40
FOLD = KT - SLOTS
WIDE = (SLOTS + 1) * TILE
BF = jnp.bfloat16


def pack_kernel(mask_ref, amps_ref, *outs):
    rows = amps_ref.shape[0]
    mask = mask_ref[...].T
    tile = lax.broadcasted_iota(jnp.int32, mask.shape, 1)
    count = jnp.sum(mask, axis=1, keepdims=True)
    low = jnp.min(jnp.where(mask > 0, tile, KT), axis=1, keepdims=True)
    high = jnp.max(jnp.where(mask > 0, tile, -1), axis=1, keepdims=True)
    end = jnp.min(jnp.where(mask > 0, KT, tile), axis=1, keepdims=True)
    wraps = high - low + 1 > count
    alpha = jnp.where(wraps, 0, jnp.minimum(low, FOLD))
    beta = jnp.where(wraps, end, SLOTS)
    first = jnp.where(wraps, end + KT - count, low)
    last = jnp.where(wraps, KT, high + 1)
    wide = lambda v: jnp.broadcast_to(v.astype(jnp.float32), (rows, TILE)).astype(BF)
    code = wide(jnp.where(wraps, -end, alpha))
    alpha, beta, first, last = wide(alpha), wide(beta), wide(first), wide(last)
    zero = jnp.zeros((rows, TILE), BF)

    def tile_of(t):
        return amps_ref[:, t * TILE : (t + 1) * TILE]

    def put(j, value):
        row = 0
        for out in outs:
            n = out.shape[0]
            out[:, j * TILE : (j + 1) * TILE] = value[row : row + n]
            row += n

    for j in range(SLOTS):
        value = jnp.where((first <= j) & (j < last), tile_of(j), zero)
        value = jnp.where((beta < SLOTS) & (j < beta), tile_of(j), value)
        far = jnp.where((first <= j + FOLD) & (j + FOLD < last), tile_of(j + FOLD), zero)
        value = jnp.where(beta <= j, far, value)
        if j < FOLD:
            up = jnp.where((first <= j + SLOTS) & (j + SLOTS < last), tile_of(j + SLOTS), zero)
            value = jnp.where(j < alpha, up, value)
        put(j, value)
    put(SLOTS, code)


def ints_kernel(mask_ref, ints_ref, kept_ref):
    for i in range(ints_ref.shape[0] // TILE):
        for j in range(ints_ref.shape[1] // TILE):
            at = (slice(i * TILE, (i + 1) * TILE), slice(j * TILE, (j + 1) * TILE))
            keep = jnp.full((TILE, TILE), mask_ref[j, i].astype(jnp.float32), jnp.float32).astype(BF)
            kept_ref[at] = ints_ref[at] * keep


def mm_kernel(spots, chunks, offs, *refs):
    n = len(spots)
    amps, ints = refs[:n], refs[n]
    out, land, wide, done, amp_sems, out_sems = refs[-6:]
    rows = amps[0].shape[0]
    place = [pl.ds(i * rows, rows) for i in range(n)]
    loads = [pltpu.make_async_copy(amps[i], land.at[place[i]], amp_sems.at[i]) for i in range(n)]
    stores = [
        pltpu.make_async_copy(done.at[place[i]], out.at[pl.ds(pl.multiple_of(offs[spots[i]], 16), rows)], out_sems.at[i])
        for i in range(n)
    ]
    for load in loads:
        load.start()

    def fill(i):
        here = slice(i * rows, (i + 1) * rows)
        code = land[here, SLOTS * TILE :]
        zero = jnp.zeros((rows, TILE), BF)
        alpha = jnp.where(code < 0, zero, code)
        beta = jnp.where(code < 0, zero - code, zero + SLOTS)

        def slot(j):
            return land[here, j * TILE : (j + 1) * TILE]

        for t in range(KT):
            if t < FOLD:
                v = jnp.where((alpha <= t) & (t < beta), slot(t), zero)
            elif t < SLOTS:
                v = jnp.where(t < beta, slot(t), zero)
                v = jnp.where(beta <= t - FOLD, slot(t - FOLD), v)
            else:
                v = jnp.where(t - SLOTS < alpha, slot(t - SLOTS), zero)
                v = jnp.where(beta <= t - FOLD, slot(t - FOLD), v)
            wide[here, t * TILE : (t + 1) * TILE] = v

    first = 0
    for size in chunks:
        for i in range(first, first + size):
            loads[i].wait()
            fill(i)
        here = slice(first * rows, (first + size) * rows)
        done[here, :] = jnp.dot(wide[here, :], ints[...], preferred_element_type=jnp.float32).astype(BF)
        for i in range(first, first + size):
            stores[i].start()
        first += size
    for store in stores:
        store.wait()


def multiply(amps, spots, chunks, offs, ints, out, out_rows):
    rows = sum(v.shape[0] for v in amps)
    cols = ints.shape[1]
    anywhere = pl.BlockSpec(memory_space=pl.ANY)
    in_specs = [pl.BlockSpec(memory_space=pltpu.SMEM)] + [anywhere] * len(amps) + [pl.BlockSpec(memory_space=pltpu.VMEM)]
    args = [offs] + list(amps) + [ints]
    alias = {}
    if out is not None:
        in_specs.append(anywhere)
        alias = {len(args): 0}
        args.append(out)
    return pl.pallas_call(
        functools.partial(mm_kernel, tuple(spots), tuple(chunks)),
        out_shape=jax.ShapeDtypeStruct((out_rows, cols), BF),
        in_specs=in_specs,
        out_specs=anywhere,
        scratch_shapes=[
            pltpu.VMEM((rows, WIDE), BF),
            pltpu.VMEM((rows, KT * TILE), BF),
            pltpu.VMEM((rows, cols), BF),
            pltpu.SemaphoreType.DMA((len(amps),)),
            pltpu.SemaphoreType.DMA((len(amps),)),
        ],
        input_output_aliases=alias,
        compiler_params=pltpu.CompilerParams(vmem_limit_bytes=16 * 2**20),
        cost_estimate=pl.CostEstimate(
            flops=2 * rows * KT * TILE * cols,
            bytes_accessed=2 * (rows * WIDE + KT * TILE * cols + rows * cols),
            transcendentals=0,
        ),
    )(*args)


def pack(mask, amps):
    rows = amps.shape[0]
    sizes = [rows]
    return pl.pallas_call(
        pack_kernel,
        out_shape=[jax.ShapeDtypeStruct((n, WIDE), BF) for n in sizes],
    )(mask.T, amps)


def mask_ints(mask, ints):
    return pl.pallas_call(
        ints_kernel,
        out_shape=jax.ShapeDtypeStruct(ints.shape, ints.dtype),
        in_specs=[pl.BlockSpec(memory_space=pltpu.SMEM), pl.BlockSpec(memory_space=pltpu.VMEM)],
        out_specs=pl.BlockSpec(memory_space=pltpu.VMEM),
    )(mask.T, ints)


def moves(n, n_row):
    def shift(dx, dz):
        pairs = []
        for r in range(n_row):
            s = 1 - 2 * (r % 2)
            for x in range(n):
                for z in range(n):
                    pairs.append(((r * n + x) * n + z, (r * n + (x + s * dx) % n) * n + (z + s * dz) % n))
        return pairs

    return shift(1, 0), shift(0, 1)


def join_kernel(offs, *refs):
    blocks, out, sems = refs[:-2], refs[-2], refs[-1]
    copies = []
    for i, block in enumerate(blocks):
        rows = block.shape[0]
        there = pl.ds(pl.multiple_of(offs[i] * rows, rows), rows)
        copies.append(pltpu.make_async_copy(block, out.at[there], sems.at[i]))
    for copy in copies:
        copy.start()
    for copy in copies:
        copy.wait()


def join(blocks, places):
    rows, cols = blocks[0].shape
    return pl.pallas_call(
        join_kernel,
        out_shape=jax.ShapeDtypeStruct((rows * len(blocks), cols), BF),
        in_specs=[pl.BlockSpec(memory_space=pltpu.SMEM)] + [pl.BlockSpec(memory_space=pl.ANY)] * len(blocks),
        out_specs=pl.BlockSpec(memory_space=pltpu.VMEM),
        scratch_shapes=[pltpu.SemaphoreType.DMA((len(blocks),))],
        compiler_params=pltpu.CompilerParams(vmem_limit_bytes=16 * 2**20),
    )(places.astype(jnp.int32), *blocks)


def after(value, *first):
    return lax.optimization_barrier((value, *first))[0]


def on_device(amplitudes, integrals, amplitude_mask, integral_mask):
    dev_rows = amplitudes.shape[0]
    own = pack(amplitude_mask, amplitudes)[0]
    kept_ints = mask_ints(integral_mask, integrals)
    row = lax.axis_index("row")
    core, y = row % 2, row // 2
    sign = 1 - 2 * core
    by_y = lambda v: lax.ppermute(v, "row", [(r, (r + (2 if r % 2 == 0 else -2)) % 8) for r in range(8)])
    swap = lambda v: lax.ppermute(v, "row", [(r, r ^ 1) for r in range(8)])
    step = jnp.arange(4)
    along_x, along_z = moves(4, 8)
    by_x = lambda v: lax.ppermute(v, ("row", "col"), along_x)
    by_z = lambda v: lax.ppermute(v, ("row", "col"), along_z)
    me = lax.axis_index("col")
    x, z = me // 4, me % 4
    spot = jnp.arange(16)
    offs = ((x - sign * (spot // 4) + 4) % 4 * 4 + (z - sign * (spot % 4) + 4) % 4) * dev_rows
    offs = offs.astype(jnp.int32)
    total = 16 * dev_rows

    b10, b01 = by_x(own), by_z(own)
    i0 = kept_ints
    i1, s0 = by_y(i0), swap(i0)
    b20, b02, b11 = by_x(after(b10, b01)), by_z(after(b01, b10)), by_x(b01)
    i2, s1 = by_y(after(i1, s0, b10, b01)), swap(i1)
    b21, b30, b03, b12 = by_z(after(b20, b02)), by_x(after(b20, b02)), by_z(b02), by_x(after(b02, b11))
    i3, s2 = by_y(after(i2, s1, b20, b02)), swap(i2)
    s3 = swap(after(i3, s2))
    b22 = by_z(after(b21, b11))
    places = jnp.concatenate([(y - sign * step + 4) % 4 * 2 + core, (y + sign * step + 4) % 4 * 2 + 1 - core])
    ints = join([i0, i1, i2, i3, s0, s1, s2, s3], places)

    b13, b31 = by_x(after(b03, b12)), by_z(after(b30, b03))
    b32, b23 = by_x(after(b22, b12)), by_z(after(b22, b03))
    b33 = by_z(b32)
    out = multiply([own, b10, b01, b20, b02], [0, 4, 1, 8, 2], [2, 3], offs, ints, None, total)
    out = multiply([b11, b21, b30, b03], [5, 9, 12, 3], [2, 2], offs, ints, out, total)
    out = multiply([b12, b22, b13, b31], [6, 10, 7, 13], [2, 2], offs, ints, out, total)
    out = multiply([b32, b23], [14, 11], [2], offs, ints, out, total)
    return multiply([b33], [15], [1], offs, ints, out, total)


def solution(mesh):
    in_specs = (P(("row", "col"), None), P("row", "col"), P(("row", "col"), None), P("row", "col"))
    out_specs = P("row", "col")
    return jax.shard_map(
        on_device, mesh=mesh, in_specs=in_specs, out_specs=out_specs, check_vma=False
    )
```

```python
import functools

import jax
import jax.numpy as jnp
from jax import lax
from jax.experimental import pallas as pl
from jax.experimental.pallas import tpu as pltpu
from jax.sharding import PartitionSpec as P

TILE = 128
KT = 64
SLOTS = 40
FOLD = KT - SLOTS
WIDE = (SLOTS + 1) * TILE
BF = jnp.bfloat16


def pack_kernel(mask_ref, amps_ref, *outs):
    rows = amps_ref.shape[0]
    mask = mask_ref[...].T
    tile = lax.broadcasted_iota(jnp.int32, mask.shape, 1)
    count = jnp.sum(mask, axis=1, keepdims=True)
    low = jnp.min(jnp.where(mask > 0, tile, KT), axis=1, keepdims=True)
    high = jnp.max(jnp.where(mask > 0, tile, -1), axis=1, keepdims=True)
    end = jnp.min(jnp.where(mask > 0, KT, tile), axis=1, keepdims=True)
    wraps = high - low + 1 > count
    alpha = jnp.where(wraps, 0, jnp.minimum(low, FOLD))
    beta = jnp.where(wraps, end, SLOTS)
    first = jnp.where(wraps, end + KT - count, low)
    last = jnp.where(wraps, KT, high + 1)
    wide = lambda v: jnp.broadcast_to(v.astype(jnp.float32), (rows, TILE)).astype(BF)
    code = wide(jnp.where(wraps, -end, alpha))
    alpha, beta, first, last = wide(alpha), wide(beta), wide(first), wide(last)
    zero = jnp.zeros((rows, TILE), BF)

    def tile_of(t):
        return amps_ref[:, t * TILE : (t + 1) * TILE]

    def put(j, value):
        row = 0
        for out in outs:
            n = out.shape[0]
            out[:, j * TILE : (j + 1) * TILE] = value[row : row + n]
            row += n

    for j in range(SLOTS):
        value = jnp.where((first <= j) & (j < last), tile_of(j), zero)
        value = jnp.where((beta < SLOTS) & (j < beta), tile_of(j), value)
        far = jnp.where((first <= j + FOLD) & (j + FOLD < last), tile_of(j + FOLD), zero)
        value = jnp.where(beta <= j, far, value)
        if j < FOLD:
            up = jnp.where((first <= j + SLOTS) & (j + SLOTS < last), tile_of(j + SLOTS), zero)
            value = jnp.where(j < alpha, up, value)
        put(j, value)
    put(SLOTS, code)


def ints_kernel(mask_ref, ints_ref, kept_ref):
    for i in range(ints_ref.shape[0] // TILE):
        for j in range(ints_ref.shape[1] // TILE):
            at = (slice(i * TILE, (i + 1) * TILE), slice(j * TILE, (j + 1) * TILE))
            keep = jnp.full((TILE, TILE), mask_ref[j, i].astype(jnp.float32), jnp.float32).astype(BF)
            kept_ref[at] = ints_ref[at] * keep


def mm_kernel(spots, chunks, offs, *refs):
    n = len(spots)
    amps, ints = refs[:n], refs[n]
    out, wide, done, out_sems = refs[-4:]
    rows = amps[0].shape[0]
    place = [pl.ds(i * rows, rows) for i in range(n)]
    stores = [
        pltpu.make_async_copy(done.at[place[i]], out.at[pl.ds(pl.multiple_of(offs[spots[i]], 16), rows)], out_sems.at[i])
        for i in range(n)
    ]
    def fill(i):
        here = slice(i * rows, (i + 1) * rows)
        code = amps[i][:, SLOTS * TILE :]
        zero = jnp.zeros((rows, TILE), BF)
        alpha = jnp.where(code < 0, zero, code)
        beta = jnp.where(code < 0, zero - code, zero + SLOTS)

        def slot(j):
            return amps[i][:, j * TILE : (j + 1) * TILE]

        for t in range(KT):
            if t < FOLD:
                v = jnp.where((alpha <= t) & (t < beta), slot(t), zero)
            elif t < SLOTS:
                v = jnp.where(t < beta, slot(t), zero)
                v = jnp.where(beta <= t - FOLD, slot(t - FOLD), v)
            else:
                v = jnp.where(t - SLOTS < alpha, slot(t - SLOTS), zero)
                v = jnp.where(beta <= t - FOLD, slot(t - FOLD), v)
            wide[here, t * TILE : (t + 1) * TILE] = v

    first = 0
    for size in chunks:
        for i in range(first, first + size):
            fill(i)
        here = slice(first * rows, (first + size) * rows)
        done[here, :] = jnp.dot(wide[here, :], ints[...], preferred_element_type=jnp.float32).astype(BF)
        for i in range(first, first + size):
            stores[i].start()
        first += size
    for store in stores:
        store.wait()


def multiply(amps, spots, chunks, offs, ints, out, out_rows):
    rows = sum(v.shape[0] for v in amps)
    cols = ints.shape[1]
    anywhere = pl.BlockSpec(memory_space=pl.ANY)
    in_specs = [pl.BlockSpec(memory_space=pltpu.SMEM)] + [pl.BlockSpec(memory_space=pltpu.VMEM)] * (len(amps) + 1)
    args = [offs] + list(amps) + [ints]
    alias = {}
    if out is not None:
        in_specs.append(anywhere)
        alias = {len(args): 0}
        args.append(out)
    return pl.pallas_call(
        functools.partial(mm_kernel, tuple(spots), tuple(chunks)),
        out_shape=jax.ShapeDtypeStruct((out_rows, cols), BF),
        in_specs=in_specs,
        out_specs=anywhere,
        scratch_shapes=[
            pltpu.VMEM((rows, KT * TILE), BF),
            pltpu.VMEM((rows, cols), BF),
            pltpu.SemaphoreType.DMA((len(amps),)),
        ],
        input_output_aliases=alias,
        compiler_params=pltpu.CompilerParams(vmem_limit_bytes=16 * 2**20),
        cost_estimate=pl.CostEstimate(
            flops=2 * rows * KT * TILE * cols,
            bytes_accessed=2 * (rows * WIDE + KT * TILE * cols + rows * cols),
            transcendentals=0,
        ),
    )(*args)


def pack(mask, amps):
    rows = amps.shape[0]
    sizes = [rows]
    return pl.pallas_call(
        pack_kernel,
        out_shape=[jax.ShapeDtypeStruct((n, WIDE), BF) for n in sizes],
    )(mask.T, amps)


def mask_ints(mask, ints):
    return pl.pallas_call(
        ints_kernel,
        out_shape=jax.ShapeDtypeStruct(ints.shape, ints.dtype),
        in_specs=[pl.BlockSpec(memory_space=pltpu.SMEM), pl.BlockSpec(memory_space=pltpu.VMEM)],
        out_specs=pl.BlockSpec(memory_space=pltpu.VMEM),
    )(mask.T, ints)


def moves(n, n_row):
    def shift(dx, dz):
        pairs = []
        for r in range(n_row):
            s = 1 - 2 * (r % 2)
            for x in range(n):
                for z in range(n):
                    pairs.append(((r * n + x) * n + z, (r * n + (x + s * dx) % n) * n + (z + s * dz) % n))
        return pairs

    return shift(1, 0), shift(0, 1)


def join_kernel(offs, *refs):
    blocks, out, sems = refs[:-2], refs[-2], refs[-1]
    copies = []
    for i, block in enumerate(blocks):
        rows = block.shape[0]
        there = pl.ds(pl.multiple_of(offs[i] * rows, rows), rows)
        copies.append(pltpu.make_async_copy(block, out.at[there], sems.at[i]))
    for copy in copies:
        copy.start()
    for copy in copies:
        copy.wait()


def join(blocks, places):
    rows, cols = blocks[0].shape
    return pl.pallas_call(
        join_kernel,
        out_shape=jax.ShapeDtypeStruct((rows * len(blocks), cols), BF),
        in_specs=[pl.BlockSpec(memory_space=pltpu.SMEM)] + [pl.BlockSpec(memory_space=pl.ANY)] * len(blocks),
        out_specs=pl.BlockSpec(memory_space=pltpu.VMEM),
        scratch_shapes=[pltpu.SemaphoreType.DMA((len(blocks),))],
        compiler_params=pltpu.CompilerParams(vmem_limit_bytes=16 * 2**20),
    )(places.astype(jnp.int32), *blocks)


def after(value, *first):
    return lax.optimization_barrier((value, *first))[0]


def on_device(amplitudes, integrals, amplitude_mask, integral_mask):
    dev_rows = amplitudes.shape[0]
    own = pack(amplitude_mask, amplitudes)[0]
    kept_ints = mask_ints(integral_mask, integrals)
    row = lax.axis_index("row")
    core, y = row % 2, row // 2
    sign = 1 - 2 * core
    by_y = lambda v: lax.ppermute(v, "row", [(r, (r + (2 if r % 2 == 0 else -2)) % 8) for r in range(8)])
    swap = lambda v: lax.ppermute(v, "row", [(r, r ^ 1) for r in range(8)])
    step = jnp.arange(4)
    along_x, along_z = moves(4, 8)
    by_x = lambda v: lax.ppermute(v, ("row", "col"), along_x)
    by_z = lambda v: lax.ppermute(v, ("row", "col"), along_z)
    me = lax.axis_index("col")
    x, z = me // 4, me % 4
    spot = jnp.arange(16)
    offs = ((x - sign * (spot // 4) + 4) % 4 * 4 + (z - sign * (spot % 4) + 4) % 4) * dev_rows
    offs = jnp.concatenate([offs, offs[15:] + dev_rows // 2]).astype(jnp.int32)
    total = 16 * dev_rows

    b10, b01 = by_x(own), by_z(own)
    i0 = kept_ints
    i1, s0 = by_y(i0), swap(i0)
    b20, b02, b11 = by_x(after(b10, b01)), by_z(after(b01, b10)), by_x(b01)
    i2, s1 = by_y(after(i1, s0, b10, b01)), swap(i1)
    b21, b30, b03, b12 = by_z(after(b20, b02)), by_x(after(b20, b02)), by_z(b02), by_x(after(b02, b11))
    i3, s2 = by_y(after(i2, s1, b20, b02)), swap(i2)
    s3 = swap(after(i3, s2, b03, b30))
    b22 = by_z(after(b21, b11))
    places = jnp.concatenate([(y - sign * step + 4) % 4 * 2 + core, (y + sign * step + 4) % 4 * 2 + 1 - core])
    ints = join([i0, i1, i2, i3, s0, s1, s2, s3], places)

    b13, b31 = by_x(after(b03, b12)), by_z(after(b30, b03))
    b32, b23 = by_x(after(b22, b12)), by_z(after(b22, b03))
    out = multiply([own, b10, b01, b20, b02], [0, 4, 1, 8, 2], [5], offs, ints, None, total)
    half = dev_rows // 2
    b32, b23, out = lax.optimization_barrier((b32, b23, out))
    b33, b33_low = by_z(b32[:half]), by_x(b23[half:])
    out = multiply([b11, b21, b30, b03, b12, b22], [5, 9, 12, 3, 6, 10], [6], offs, ints, out, total)
    out = multiply([b13, b31, b32, b23], [7, 13, 14, 11], [4], offs, ints, out, total)
    return multiply([b33, b33_low], [15, 16], [2], offs, ints, out, total)


def solution(mesh):
    in_specs = (P(("row", "col"), None), P("row", "col"), P(("row", "col"), None), P("row", "col"))
    out_specs = P("row", "col")
    return jax.shard_map(
        on_device, mesh=mesh, in_specs=in_specs, out_specs=out_specs, check_vma=False
    )
```

```python
import functools

import jax
import jax.numpy as jnp
from jax import lax
from jax.experimental import pallas as pl
from jax.experimental.pallas import tpu as pltpu
from jax.sharding import PartitionSpec as P

TILE = 128
KT = 64
SLOTS = 40
FOLD = KT - SLOTS
WIDE = (SLOTS + 1) * TILE
BF = jnp.bfloat16


def pack_kernel(mask_ref, amps_ref, *outs):
    rows = amps_ref.shape[0]
    mask = mask_ref[...].T
    tile = lax.broadcasted_iota(jnp.int32, mask.shape, 1)
    count = jnp.sum(mask, axis=1, keepdims=True)
    low = jnp.min(jnp.where(mask > 0, tile, KT), axis=1, keepdims=True)
    high = jnp.max(jnp.where(mask > 0, tile, -1), axis=1, keepdims=True)
    end = jnp.min(jnp.where(mask > 0, KT, tile), axis=1, keepdims=True)
    wraps = high - low + 1 > count
    alpha = jnp.where(wraps, 0, jnp.minimum(low, FOLD))
    beta = jnp.where(wraps, end, SLOTS)
    first = jnp.where(wraps, end + KT - count, low)
    last = jnp.where(wraps, KT, high + 1)
    wide = lambda v: jnp.broadcast_to(v.astype(jnp.float32), (rows, TILE)).astype(BF)
    code = wide(jnp.where(wraps, -end, alpha))
    alpha, beta, first, last = wide(alpha), wide(beta), wide(first), wide(last)
    zero = jnp.zeros((rows, TILE), BF)

    def tile_of(t):
        return amps_ref[:, t * TILE : (t + 1) * TILE]

    def put(j, value):
        row = 0
        for out in outs:
            n = out.shape[0]
            out[:, j * TILE : (j + 1) * TILE] = value[row : row + n]
            row += n

    for j in range(SLOTS):
        value = jnp.where((first <= j) & (j < last), tile_of(j), zero)
        value = jnp.where((beta < SLOTS) & (j < beta), tile_of(j), value)
        far = jnp.where((first <= j + FOLD) & (j + FOLD < last), tile_of(j + FOLD), zero)
        value = jnp.where(beta <= j, far, value)
        if j < FOLD:
            up = jnp.where((first <= j + SLOTS) & (j + SLOTS < last), tile_of(j + SLOTS), zero)
            value = jnp.where(j < alpha, up, value)
        put(j, value)
    put(SLOTS, code)


def ints_kernel(mask_ref, ints_ref, kept_ref):
    for i in range(ints_ref.shape[0] // TILE):
        for j in range(ints_ref.shape[1] // TILE):
            at = (slice(i * TILE, (i + 1) * TILE), slice(j * TILE, (j + 1) * TILE))
            keep = jnp.full((TILE, TILE), mask_ref[j, i].astype(jnp.float32), jnp.float32).astype(BF)
            kept_ref[at] = ints_ref[at] * keep


def mm_kernel(spots, offs, *refs):
    n = len(spots)
    amps, ints = refs[:n], refs[n]
    out, wide, done, out_sems = refs[-4:]
    sizes = [v.shape[0] for v in amps]
    begin = [sum(sizes[:i]) for i in range(n)]
    place = [pl.ds(begin[i], sizes[i]) for i in range(n)]
    stores = [
        pltpu.make_async_copy(done.at[place[i]], out.at[pl.ds(pl.multiple_of(offs[spots[i]], 16), sizes[i])], out_sems.at[i])
        for i in range(n)
    ]
    def fill(i):
        rows = sizes[i]
        here = slice(begin[i], begin[i] + rows)
        code = amps[i][:, SLOTS * TILE :]
        zero = jnp.zeros((rows, TILE), BF)
        alpha = jnp.where(code < 0, zero, code)
        beta = jnp.where(code < 0, zero - code, zero + SLOTS)

        def slot(j):
            return amps[i][:, j * TILE : (j + 1) * TILE]

        for t in range(KT):
            if t < FOLD:
                v = jnp.where((alpha <= t) & (t < beta), slot(t), zero)
            elif t < SLOTS:
                v = jnp.where(t < beta, slot(t), zero)
                v = jnp.where(beta <= t - FOLD, slot(t - FOLD), v)
            else:
                v = jnp.where(t - SLOTS < alpha, slot(t - SLOTS), zero)
                v = jnp.where(beta <= t - FOLD, slot(t - FOLD), v)
            wide[here, t * TILE : (t + 1) * TILE] = v

    for i in range(n):
        fill(i)
    done[...] = jnp.dot(wide[...], ints[...], preferred_element_type=jnp.float32).astype(BF)
    for store in stores:
        store.start()
    for store in stores:
        store.wait()


def multiply(amps, spots, offs, ints, out, out_rows):
    rows = sum(v.shape[0] for v in amps)
    cols = ints.shape[1]
    anywhere = pl.BlockSpec(memory_space=pl.ANY)
    in_specs = [pl.BlockSpec(memory_space=pltpu.SMEM)] + [pl.BlockSpec(memory_space=pltpu.VMEM)] * (len(amps) + 1)
    args = [offs] + list(amps) + [ints]
    alias = {}
    if out is not None:
        in_specs.append(anywhere)
        alias = {len(args): 0}
        args.append(out)
    return pl.pallas_call(
        functools.partial(mm_kernel, tuple(spots)),
        out_shape=jax.ShapeDtypeStruct((out_rows, cols), BF),
        in_specs=in_specs,
        out_specs=anywhere,
        scratch_shapes=[
            pltpu.VMEM((rows, KT * TILE), BF),
            pltpu.VMEM((rows, cols), BF),
            pltpu.SemaphoreType.DMA((len(amps),)),
        ],
        input_output_aliases=alias,
        compiler_params=pltpu.CompilerParams(vmem_limit_bytes=30 * 2**20),
        cost_estimate=pl.CostEstimate(
            flops=2 * rows * KT * TILE * cols,
            bytes_accessed=2 * (rows * WIDE + KT * TILE * cols + rows * cols),
            transcendentals=0,
        ),
    )(*args)


def pack(mask, amps):
    rows = amps.shape[0]
    sizes = [rows]
    return pl.pallas_call(
        pack_kernel,
        out_shape=[jax.ShapeDtypeStruct((n, WIDE), BF) for n in sizes],
    )(mask.T, amps)


def mask_ints(mask, ints):
    return pl.pallas_call(
        ints_kernel,
        out_shape=jax.ShapeDtypeStruct(ints.shape, ints.dtype),
        in_specs=[pl.BlockSpec(memory_space=pltpu.SMEM), pl.BlockSpec(memory_space=pltpu.VMEM)],
        out_specs=pl.BlockSpec(memory_space=pltpu.VMEM),
    )(mask.T, ints)


def moves(n, n_row):
    def shift(dx, dz):
        pairs = []
        for r in range(n_row):
            s = 1 - 2 * (r % 2)
            for x in range(n):
                for z in range(n):
                    pairs.append(((r * n + x) * n + z, (r * n + (x + s * dx) % n) * n + (z + s * dz) % n))
        return pairs

    return shift(1, 0), shift(0, 1)


def join_kernel(offs, *refs):
    blocks, out, sems = refs[:-2], refs[-2], refs[-1]
    copies = []
    for i, block in enumerate(blocks):
        rows = block.shape[0]
        there = pl.ds(pl.multiple_of(offs[i] * rows, rows), rows)
        copies.append(pltpu.make_async_copy(block, out.at[there], sems.at[i]))
    for copy in copies:
        copy.start()
    for copy in copies:
        copy.wait()


def join(blocks, places):
    rows, cols = blocks[0].shape
    return pl.pallas_call(
        join_kernel,
        out_shape=jax.ShapeDtypeStruct((rows * len(blocks), cols), BF),
        in_specs=[pl.BlockSpec(memory_space=pltpu.SMEM)] + [pl.BlockSpec(memory_space=pl.ANY)] * len(blocks),
        out_specs=pl.BlockSpec(memory_space=pltpu.VMEM),
        scratch_shapes=[pltpu.SemaphoreType.DMA((len(blocks),))],
        compiler_params=pltpu.CompilerParams(vmem_limit_bytes=16 * 2**20),
    )(places.astype(jnp.int32), *blocks)


def after(value, *first):
    return lax.optimization_barrier((value, *first))[0]


def on_device(amplitudes, integrals, amplitude_mask, integral_mask):
    dev_rows = amplitudes.shape[0]
    own = pack(amplitude_mask, amplitudes)[0]
    kept_ints = mask_ints(integral_mask, integrals)
    row = lax.axis_index("row")
    core, y = row % 2, row // 2
    sign = 1 - 2 * core
    by_y = lambda v: lax.ppermute(v, "row", [(r, (r + (2 if r % 2 == 0 else -2)) % 8) for r in range(8)])
    swap = lambda v: lax.ppermute(v, "row", [(r, r ^ 1) for r in range(8)])
    step = jnp.arange(4)
    along_x, along_z = moves(4, 8)
    by_x = lambda v: lax.ppermute(v, ("row", "col"), along_x)
    by_z = lambda v: lax.ppermute(v, ("row", "col"), along_z)
    me = lax.axis_index("col")
    x, z = me // 4, me % 4
    spot = jnp.arange(16)
    offs = ((x - sign * (spot // 4) + 4) % 4 * 4 + (z - sign * (spot % 4) + 4) % 4) * dev_rows
    offs = jnp.concatenate([offs, offs[15:] + dev_rows // 2]).astype(jnp.int32)
    total = 16 * dev_rows

    b10, b01 = by_x(own), by_z(own)
    i0 = kept_ints
    i1, s0 = by_y(i0), swap(i0)
    b20, b02, b11 = by_x(after(b10, b01)), by_z(after(b01, b10)), by_x(b01)
    i2, s1 = by_y(after(i1, s0, b10, b01)), swap(i1)
    b21, b30, b03, b12 = by_z(after(b20, b02)), by_x(after(b20, b02)), by_z(b02), by_x(after(b02, b11))
    i3, s2 = by_y(after(i2, s1, b20, b02)), swap(i2)
    s3 = swap(after(i3, s2, b03, b30))
    b22 = by_z(after(b21, b11))
    places = jnp.concatenate([(y - sign * step + 4) % 4 * 2 + core, (y + sign * step + 4) % 4 * 2 + 1 - core])
    ints = join([i0, i1, i2, i3, s0, s1, s2, s3], places)

    b13, b31 = by_x(after(b03, b12)), by_z(after(b30, b03))
    b32, b23 = by_x(after(b22, b12)), by_z(after(b22, b03))
    out = multiply([own, b10, b01, b20, b02], [0, 4, 1, 8, 2], offs, ints, None, total)
    half = dev_rows // 2
    b32, b23, out = lax.optimization_barrier((b32, b23, out))
    b33, b33_low = by_z(b32[:half]), by_x(b23[half:])
    out = multiply([b11, b21, b30, b03, b12, b22, b32, b23], [5, 9, 12, 3, 6, 10, 14, 11], offs, ints, out, total)
    return multiply([b13, b31, b33, b33_low], [7, 13, 15, 16], offs, ints, out, total)


def solution(mesh):
    in_specs = (P(("row", "col"), None), P("row", "col"), P(("row", "col"), None), P("row", "col"))
    out_specs = P("row", "col")
    return jax.shard_map(
        on_device, mesh=mesh, in_specs=in_specs, out_specs=out_specs, check_vma=False
    )
```
